512 devices in a mesh: row: 16 (over y, z_hi, core), col: 32 (over x, z_lo).
Axes of the slice: x: 4, y: 4, z: 16 (z_hi: 2, z_lo: 8; z = z_hi * 8 + z_lo), core: 2. Of those that a mesh axis runs over, the one named last changes fastest.
Arguments:
- observed: bfloat16 [32768, 128], P(('row', 'col')), may hold values from -6 to 6
- prior_mean: bfloat16 [32768, 128], P(('row', 'col')), may hold values from -6 to 6
- missing: int32 [32768, 128], P(('row', 'col')), may hold values 0 or 1
- eigvec: bfloat16 [32768, 32768], P('row', 'col'), may hold values from -0.0625 to 0.0625
- lam_space: float32 [32768], P('col'), may hold values from 0.1 to 10
- lam_time: float32 [32], replicated, may hold values from 0.1 to 10
Outputs:
- smoothed: float32 [32768, 128], P(('row', 'col'))
The draws below stay inside these ranges and needn't reach their ends.
All inputs are finite; a program needn't handle non-finite values. No bound on the sum of `missing` on one device may be relied on, other than what follows from the above.
Results may differ from the reference program's by a relative error of at most 0.0022.
Values may be sent and summed in bfloat16 or wider, within the bound.
No kernel may reach another device: no remote copies, remote signals or barrier semaphores. Data moves between devices by JAX's collectives and lax.ppermute only.
A program may use at most 64 MiB of HBM per device.

```python
import math
import jax
import jax.numpy as jnp
from jax import lax

MONTHS = 32
VARS = 4
STATIONS = 32768
EIGS = 32768
COLS = 128


def touch_ends(entries, stream_key, low, top_value):
    extent = entries.shape
    place = [jax.random.randint(jax.random.fold_in(stream_key, axis), (), 0, extent[axis]) for axis in range(len(extent))]
    entries = entries.at[tuple(place)].set(low)
    longest = extent.index(max(extent))
    place[longest] = (place[longest] + 1) % extent[longest]
    return entries.at[tuple(place)].set(top_value)


def strengthened(array, rng, source, target, shards_of, factor):
    owner, partner = [(jnp.arange(array.shape[position]) // (array.shape[position] // shards_of)).reshape([-1 if axis == position else 1 for axis in range(array.ndim)]) for position in (source, target)]
    chosen = jax.random.permutation(rng, shards_of)[partner]
    strong = (owner == chosen) | (owner == (partner + shards_of // 2) % shards_of)
    return jnp.where(strong, factor * array, array)


def block_scale(rng, extent, pieces, smallest, largest):
    def one(position, shards_of):
        draws = jax.random.uniform(jax.random.fold_in(jax.random.fold_in(rng, 6), position), (shards_of,), jnp.float32, smallest / len(pieces), largest / len(pieces))
        return jnp.repeat(jnp.exp(draws), extent[position] // shards_of).reshape((-1,) + (1,) * (len(extent) - position - 1))

    level = one(*pieces[0])
    for cut in pieces[1:]:
        level = level * one(*cut)
    return level


def centred(rng, dims, scale, limit, cuts=(), kind=jnp.bfloat16):
    entries = scale * jax.random.normal(rng, dims, jnp.float32)
    if cuts:
        entries = entries * block_scale(rng, dims, cuts, -0.22, 0.18)
    return jnp.clip(entries, -limit, limit).astype(kind)


def gaussian_with(key, dims, width, limit, shards, heavy, held_as=jnp.bfloat16):
    values = width * jax.random.normal(key, dims, jnp.float32)
    if shards:
        values = values * block_scale(key, dims, shards, -0.22, 0.18)
    return jnp.clip(strengthened(values, jax.random.fold_in(key, 3), *heavy), -limit, limit).astype(held_as)


def setup_inputs(seed: int = 0) -> dict:
    streams_of = jax.random.split(jax.random.key(seed), 7)
    return {
        "observed": centred(streams_of[0], (STATIONS, COLS), 1.0, 6.0, ((0, 512),)),
        "prior_mean": centred(streams_of[1], (STATIONS, COLS), 1.0, 6.0, ((0, 512),)),
        "missing": touch_ends((jax.random.randint(streams_of[2], (STATIONS, COLS), 0, 3) < 1).astype(jnp.int32), jax.random.fold_in(streams_of[2], 1), 0, 1),
        "eigvec": gaussian_with(streams_of[3], (STATIONS, EIGS), STATIONS ** -0.5, 0.0625, ((0, 16), (1, 32)), (1, 0, 32, 2.75)),
        "lam_space": jnp.clip(jnp.exp(math.log(10.0) - 4.6051702 * jax.random.uniform(streams_of[4], (EIGS,), jnp.float32) ** block_scale(streams_of[4], (EIGS,), ((0, 32),), -0.2, 0.2)), 0.1, 10.0),
        "lam_time": jnp.clip(jnp.exp(jax.random.uniform(streams_of[5], (MONTHS,), jnp.float32, math.log(0.1), math.log(10.0))), 0.1, 10.0),
    }


def cosine_table():
    freq = jnp.arange(MONTHS, dtype=jnp.float32)[:, None]
    month = jnp.arange(MONTHS, dtype=jnp.float32)[None, :]
    table = jnp.cos(math.pi * (month + 0.5) * freq / MONTHS) * math.sqrt(2.0 / MONTHS)
    first = jnp.where(jnp.arange(MONTHS)[:, None] == 0, 1.0 / math.sqrt(2.0), 1.0)
    return (table * first).astype(jnp.float32)

def shrink(proj, lam_space, lam_time):
    count = proj.shape[0]
    table = cosine_table()
    blocks = proj.reshape(count, VARS, MONTHS)
    spec = jnp.einsum('kvm,jm->kvj', blocks, table, precision=lax.Precision.HIGHEST)
    gain = lam_space[:, None] * lam_time[None, :]
    gain = gain / (gain + 1.0)
    scaled = spec * gain[:, None, :]
    back = jnp.einsum('kvj,jm->kvm', scaled, table, precision=lax.Precision.HIGHEST)
    return back.reshape(count, VARS * MONTHS).astype(jnp.bfloat16)

def reference(observed, prior_mean, missing, eigvec, lam_space, lam_time):
    filled = jnp.where(missing == 1, prior_mean, observed)
    proj = lax.dot_general(eigvec, filled, (((0,), (0,)), ((), ())), preferred_element_type=jnp.float32)
    coeffs = shrink(proj, lam_space, lam_time)
    return jnp.dot(eigvec, coeffs, preferred_element_type=jnp.float32)
```

```python
import math

import jax
import jax.numpy as jnp
from jax import lax
from jax.sharding import Mesh
from jax.sharding import PartitionSpec as P

MONTHS = 32
VARS = 4
ROW = ("y", "zh", "core")
COL = ("x", "zl")
PAIR = ("y", "core")


def cosine_table():
    freq = jnp.arange(MONTHS, dtype=jnp.float32)[:, None]
    month = jnp.arange(MONTHS, dtype=jnp.float32)[None, :]
    table = jnp.cos(math.pi * (month + 0.5) * freq / MONTHS) * math.sqrt(2.0 / MONTHS)
    first = jnp.where(jnp.arange(MONTHS)[:, None] == 0, 1.0 / math.sqrt(2.0), 1.0)
    return table * first


def shrink(proj, lam_space, lam_time):
    count = proj.shape[0]
    table = cosine_table()
    blocks = proj.reshape(count, VARS, MONTHS)
    spec = jnp.einsum("kvm,jm->kvj", blocks, table, precision=lax.Precision.HIGHEST)
    gain = lam_space[:, None] * lam_time[None, :]
    gain = gain / (gain + 1.0)
    scaled = spec * gain[:, None, :]
    back = jnp.einsum("kvj,jm->kvm", scaled, table, precision=lax.Precision.HIGHEST)
    return back.reshape(count, VARS * MONTHS).astype(jnp.bfloat16)


def gather(block, axes):
    size = lax.axis_size(axes)
    copies = jnp.broadcast_to(block, (size,) + block.shape)
    return lax.all_to_all(copies, axes, 0, 0).reshape((size * block.shape[0],) + block.shape[1:])


def scatter_sum(parts, axes):
    size = lax.axis_size(axes)
    pieces = parts.reshape((size, parts.shape[0] // size) + parts.shape[1:])
    return lax.all_to_all(pieces, axes, 0, 0).astype(jnp.float32).sum(0)


def shards(observed, prior_mean, missing, eigvec, lam_space, lam_time):
    filled = jnp.where(missing == 1, prior_mean, observed)
    filled = gather(gather(filled, "zl"), "x")
    proj = lax.dot_general(eigvec, filled, (((0,), (0,)), ((), ())), preferred_element_type=jnp.float32)
    total = scatter_sum(proj, PAIR)
    total = total + lax.ppermute(total, "zh", [(0, 1), (1, 0)])
    count = total.shape[0]
    mine = lax.dynamic_slice_in_dim(lam_space, lax.axis_index(PAIR) * count, count)
    coeffs = gather(shrink(total, mine, lam_time), PAIR)
    part = jnp.dot(eigvec, coeffs, preferred_element_type=jnp.float32).astype(jnp.bfloat16)
    return scatter_sum(scatter_sum(part, "x"), "zl")


def solution(mesh):
    fine = Mesh(mesh.devices.reshape(4, 2, 2, 4, 8), ("y", "zh", "core", "x", "zl"))
    rows = P(ROW + COL, None)
    in_specs = (rows, rows, rows, P(ROW, COL), P(COL), P())
    return jax.shard_map(shards, mesh=fine, in_specs=in_specs, out_specs=rows, check_vma=False)
```

```python
import math

import jax
import jax.numpy as jnp
import numpy as np
from jax import lax
from jax.experimental import pallas as pl
from jax.experimental.pallas import tpu as pltpu
from jax.sharding import Mesh
from jax.sharding import PartitionSpec as P

MONTHS = 32
VARS = 4
COLS = MONTHS * VARS
ROW = ("y", "zh", "core")
COL = ("x", "zl")
EXTRA = 8
TOP = 14
VMEM = pl.BlockSpec(memory_space=pltpu.VMEM)
ANY = pl.BlockSpec(memory_space=pl.ANY)


def cosine_blocks():
    freq = np.arange(MONTHS)[:, None]
    month = np.arange(MONTHS)[None, :]
    table = np.cos(math.pi * (month + 0.5) * freq / MONTHS) * math.sqrt(2.0 / MONTHS)
    table[0] /= math.sqrt(2.0)
    return np.kron(np.eye(VARS), table).astype(np.float32)


def kernel_call(body, out_shape, in_specs, flops, nbytes, scratch_shapes=()):
    return pl.pallas_call(
        body,
        out_shape=out_shape,
        in_specs=in_specs,
        out_specs=VMEM,
        scratch_shapes=scratch_shapes,
        compiler_params=pltpu.CompilerParams(vmem_limit_bytes=12 * 2**20),
        cost_estimate=pl.CostEstimate(flops=flops, bytes_accessed=nbytes, transcendentals=0),
    )


def fetched(source, held, sem):
    copy = pltpu.make_async_copy(source, held, sem)
    copy.start()
    copy.wait()
    return held[...]


def scaled(values):
    largest = jnp.maximum(jnp.max(jnp.abs(values), keepdims=True), 1e-30)
    exponent = jnp.floor(jnp.log(largest) * (1 / math.log(2.0))) - TOP
    return values * jnp.exp2(-exponent), exponent


def put_exponent(out, exponent):
    rows = out.shape[1] - EXTRA
    out[:, rows:, :] = jnp.broadcast_to(exponent.reshape(1, 1, 1), (out.shape[0], EXTRA, out.shape[2]))


def split_kernel(proj, out):
    proj, exponent = scaled(proj[...])
    size = out.shape[2]
    for piece in range(out.shape[0]):
        out[piece, :COLS, :] = proj[:, piece * size : (piece + 1) * size]
    put_exponent(out, exponent)


def pair_kernel(pair, out):
    total, exponent = scaled(pair[0] + pair[1])
    out[0, :COLS, :] = total
    put_exponent(out, exponent)


def shrink_kernel(halves, table, lam_space, lam_time, out):
    total = sum(halves[half, :COLS, :] * jnp.exp2(halves[half, COLS : COLS + 1, :]) for half in range(halves.shape[0]))
    diagonal = lax.broadcasted_iota(jnp.int32, (MONTHS, MONTHS), 0) == lax.broadcasted_iota(jnp.int32, (MONTHS, MONTHS), 1)
    time = jnp.sum(jnp.where(diagonal, lam_time[...], 0.0), axis=1, keepdims=True)
    lines = total.shape[1] // lam_space.shape[1]
    space = [lam_space[pl.ds(lax.axis_index("y") * lines + line, 1), :] for line in range(lines)]
    gain = jnp.concatenate([time] * VARS, axis=0) * jnp.concatenate(space, axis=1)
    gain = gain / (gain + 1.0)
    spec = jnp.dot(table[...], total, precision=lax.Precision.HIGHEST, preferred_element_type=jnp.float32)
    back = lax.dot_general(
        spec * gain,
        table[...],
        (((0,), (0,)), ((), ())),
        precision=lax.Precision.HIGHEST,
        preferred_element_type=jnp.float32,
    )
    out[...] = back.astype(jnp.bfloat16)


def smooth_kernel(eigvec, coeffs, out, held, sem):
    out[...] = jnp.dot(fetched(eigvec, held, sem), coeffs[...], preferred_element_type=jnp.float32).astype(jnp.bfloat16)


def join_kernel(parts, out):
    total = parts[0].astype(jnp.float32)
    for peer in range(1, parts.shape[0]):
        total = total + parts[peer].astype(jnp.float32)
    total, exponent = scaled(total)
    size = out.shape[1] - EXTRA
    for piece in range(out.shape[0]):
        out[piece, :size, :] = total[piece * size : (piece + 1) * size]
    put_exponent(out, exponent)


def gather(block, axes):
    size = lax.axis_size(axes)
    copies = jnp.broadcast_to(block, (size,) + block.shape)
    return lax.all_to_all(copies, axes, 0, 0).reshape((size * block.shape[0],) + block.shape[1:])


def exchange_sum(pieces, axes):
    got = lax.all_to_all(pieces.astype(jnp.float16), axes, 0, 0).astype(jnp.float32)
    rows = got.shape[1] - EXTRA
    return (got[:, :rows] * jnp.exp2(got[:, rows : rows + 1])).sum(0)


def shards(observed, prior_mean, missing, eigvec, lam_space, lam_time):
    stations, eigs = eigvec.shape
    pieces = lax.axis_size("y")
    share = eigs // pieces
    flops = 2 * stations * eigs * COLS
    nbytes = 2 * stations * eigs
    filled = jnp.where(missing == 1, prior_mean, observed)
    filled = gather(gather(filled, "zl"), "x")
    proj = lax.dot_general(filled, eigvec, (((0,), (0,)), ((), ())), preferred_element_type=jnp.float32)
    split = kernel_call(
        split_kernel, jax.ShapeDtypeStruct((pieces, COLS + EXTRA, share), jnp.float32), [VMEM], eigs * COLS, 8 * eigs * COLS
    )(proj)
    pair = lax.all_gather(exchange_sum(split, "y"), "core")
    half = kernel_call(
        pair_kernel, jax.ShapeDtypeStruct((1, COLS + EXTRA, share), jnp.float32), [VMEM], share * COLS, 12 * share * COLS
    )(pair)
    halves = lax.all_gather(half.astype(jnp.float16), "zh", axis=0, tiled=True).astype(jnp.float32)
    coeffs = kernel_call(
        shrink_kernel, jax.ShapeDtypeStruct((share, COLS), jnp.bfloat16), [VMEM] * 4, 4 * COLS * COLS * share, COLS * COLS * 8
    )(halves, cosine_blocks(), lam_space.reshape(-1, COLS), lam_time.reshape(1, MONTHS))
    scratch = [pltpu.VMEM(eigvec.shape, eigvec.dtype), pltpu.SemaphoreType.DMA]
    part = kernel_call(
        smooth_kernel, jax.ShapeDtypeStruct((stations, COLS), jnp.bfloat16), [ANY, VMEM], flops, nbytes, scratch
    )(eigvec, gather(coeffs, "y"))
    across, along = lax.axis_size("x"), lax.axis_size("zl")
    parts = lax.all_to_all(part.reshape(across, stations // across, COLS), "x", 0, 0)
    joined = kernel_call(
        join_kernel,
        jax.ShapeDtypeStruct((along, stations // across // along + EXTRA, COLS), jnp.float32),
        [VMEM],
        stations * COLS,
        4 * stations * COLS,
    )(parts)
    return exchange_sum(joined, "zl")


def solution(mesh):
    fine = Mesh(mesh.devices.reshape(4, 2, 2, 4, 8), ("y", "zh", "core", "x", "zl"))
    rows = P(ROW + COL, None)
    in_specs = (rows, rows, rows, P(ROW, COL), P(COL), P())
    return jax.shard_map(shards, mesh=fine, in_specs=in_specs, out_specs=rows, check_vma=False)
```

```python
import math

import jax
import jax.numpy as jnp
import numpy as np
from jax import lax
from jax.experimental import pallas as pl
from jax.experimental.pallas import tpu as pltpu
from jax.sharding import Mesh
from jax.sharding import PartitionSpec as P

MONTHS = 32
VARS = 4
COLS = MONTHS * VARS
ROW = ("y", "zh", "core")
COL = ("x", "zl")
PAIR = ("y", "core")
EXTRA = 8
TOP = 14
VMEM = pl.BlockSpec(memory_space=pltpu.VMEM)
ANY = pl.BlockSpec(memory_space=pl.ANY)


def cosine_blocks():
    freq = np.arange(MONTHS)[:, None]
    month = np.arange(MONTHS)[None, :]
    table = np.cos(math.pi * (month + 0.5) * freq / MONTHS) * math.sqrt(2.0 / MONTHS)
    table[0] /= math.sqrt(2.0)
    return np.kron(np.eye(VARS), table).astype(np.float32)


def kernel_call(body, out_shape, in_specs, flops, nbytes, scratch_shapes=()):
    return pl.pallas_call(
        body,
        out_shape=out_shape,
        in_specs=in_specs,
        out_specs=VMEM,
        scratch_shapes=scratch_shapes,
        compiler_params=pltpu.CompilerParams(vmem_limit_bytes=12 * 2**20),
        cost_estimate=pl.CostEstimate(flops=flops, bytes_accessed=nbytes, transcendentals=0),
    )


def fetched(source, held, sem):
    copy = pltpu.make_async_copy(source, held, sem)
    copy.start()
    copy.wait()
    return held[...]


def scaled(values):
    largest = jnp.maximum(jnp.max(jnp.abs(values), keepdims=True), 1e-30)
    exponent = jnp.floor(jnp.log(largest) * (1 / math.log(2.0))) - TOP
    return values * jnp.exp2(-exponent), exponent


def put_exponent(out, exponent):
    rows = out.shape[1] - EXTRA
    out[:, rows:, :] = jnp.broadcast_to(exponent.reshape(1, 1, 1), (out.shape[0], EXTRA, out.shape[2]))


def split_kernel(proj, out):
    proj, exponent = scaled(proj[...])
    size = out.shape[2]
    for piece in range(out.shape[0]):
        out[piece, :COLS, :] = proj[:, piece * size : (piece + 1) * size]
    put_exponent(out, exponent)


def shrink_kernel(halves, table, lam_space, lam_time, out):
    total = sum(halves[half, :COLS, :] * jnp.exp2(halves[half, COLS : COLS + 1, :]) for half in range(halves.shape[0]))
    diagonal = lax.broadcasted_iota(jnp.int32, (MONTHS, MONTHS), 0) == lax.broadcasted_iota(jnp.int32, (MONTHS, MONTHS), 1)
    time = jnp.sum(jnp.where(diagonal, lam_time[...], 0.0), axis=1, keepdims=True)
    lines = total.shape[1] // lam_space.shape[1]
    space = [lam_space[pl.ds(lax.axis_index(PAIR) * lines + line, 1), :] for line in range(lines)]
    gain = jnp.concatenate([time] * VARS, axis=0) * jnp.concatenate(space, axis=1)
    gain = gain / (gain + 1.0)
    spec = jnp.dot(table[...], total, precision=lax.Precision.HIGHEST, preferred_element_type=jnp.float32)
    back = lax.dot_general(
        spec * gain,
        table[...],
        (((0,), (0,)), ((), ())),
        precision=lax.Precision.HIGHEST,
        preferred_element_type=jnp.float32,
    )
    out[...] = back.astype(jnp.bfloat16)


def smooth_kernel(eigvec, coeffs, out, held, sem):
    part, exponent = scaled(jnp.dot(fetched(eigvec, held, sem), coeffs[...], preferred_element_type=jnp.float32))
    size = out.shape[1] - EXTRA
    for piece in range(out.shape[0]):
        out[piece, :size, :] = part[piece * size : (piece + 1) * size]
    put_exponent(out, exponent)


def gather(block, axes):
    size = lax.axis_size(axes)
    copies = jnp.broadcast_to(block, (size,) + block.shape)
    return lax.all_to_all(copies, axes, 0, 0).reshape((size * block.shape[0],) + block.shape[1:])


def exchange(pieces, axes):
    got = lax.all_to_all(pieces.astype(jnp.float16), axes, 0, 0).astype(jnp.float32)
    rows = got.shape[1] - EXTRA
    return got[:, :rows], got[:, rows : rows + 1]


def shards(observed, prior_mean, missing, eigvec, lam_space, lam_time):
    stations, eigs = eigvec.shape
    pieces = lax.axis_size(PAIR)
    share = eigs // pieces
    flops = 2 * stations * eigs * COLS
    nbytes = 2 * stations * eigs
    filled = jnp.where(missing == 1, prior_mean, observed)
    filled = gather(gather(filled, "zl"), "x")
    proj = lax.dot_general(filled, eigvec, (((0,), (0,)), ((), ())), preferred_element_type=jnp.float32)
    split = kernel_call(
        split_kernel, jax.ShapeDtypeStruct((pieces, COLS + EXTRA, share), jnp.float32), [VMEM], eigs * COLS, 8 * eigs * COLS
    )(proj)
    terms, exponents = exchange(split, PAIR)
    top = exponents.max(0) + math.log2(pieces)
    half = jnp.concatenate([(terms * jnp.exp2(exponents - top)).sum(0), jnp.broadcast_to(top, (EXTRA, share))])
    halves = lax.all_gather(half.astype(jnp.float16), "zh").astype(jnp.float32)
    coeffs = kernel_call(
        shrink_kernel, jax.ShapeDtypeStruct((share, COLS), jnp.bfloat16), [VMEM] * 4, 4 * COLS * COLS * share, COLS * COLS * 8
    )(halves, cosine_blocks(), lam_space.reshape(-1, COLS), lam_time.reshape(1, MONTHS))
    scratch = [pltpu.VMEM(eigvec.shape, eigvec.dtype), pltpu.SemaphoreType.DMA]
    across, along = lax.axis_size("x"), lax.axis_size("zl")
    part = kernel_call(
        smooth_kernel,
        jax.ShapeDtypeStruct((across, stations // across + EXTRA, COLS), jnp.float32),
        [ANY, VMEM],
        flops,
        nbytes,
        scratch,
    )(eigvec, gather(coeffs, PAIR))
    terms, exponents = exchange(part, "x")
    joined = (terms * jnp.exp2(exponents)).sum(0).astype(jnp.bfloat16).reshape(along, -1, COLS)
    return lax.all_to_all(joined, "zl", 0, 0).astype(jnp.float32).sum(0)


def solution(mesh):
    fine = Mesh(mesh.devices.reshape(4, 2, 2, 4, 8), ("y", "zh", "core", "x", "zl"))
    rows = P(ROW + COL, None)
    in_specs = (rows, rows, rows, P(ROW, COL), P(COL), P())
    return jax.shard_map(shards, mesh=fine, in_specs=in_specs, out_specs=rows, check_vma=False)
```

```python
import functools
import math

import jax
import jax.numpy as jnp
import numpy as np
from jax import lax
from jax.experimental import pallas as pl
from jax.experimental.pallas import tpu as pltpu
from jax.sharding import Mesh
from jax.sharding import PartitionSpec as P

MONTHS = 32
VARS = 4
COLS = MONTHS * VARS
ROW = ("y", "zh", "core")
COL = ("x", "za", "zc")
NEAR = ("x", "zc")
PAIR = ("y", "core")
EXTRA = 8
TOP = 14
VMEM = pl.BlockSpec(memory_space=pltpu.VMEM)
ANY = pl.BlockSpec(memory_space=pl.ANY)


def cosine_blocks():
    freq = np.arange(MONTHS)[:, None]
    month = np.arange(MONTHS)[None, :]
    table = np.cos(math.pi * (month + 0.5) * freq / MONTHS) * math.sqrt(2.0 / MONTHS)
    table[0] /= math.sqrt(2.0)
    return np.kron(np.eye(VARS), table).astype(np.float32)


def kernel_call(body, out_shape, in_specs, flops, nbytes, scratch_shapes=()):
    return pl.pallas_call(
        body,
        out_shape=out_shape,
        in_specs=in_specs,
        out_specs=VMEM,
        scratch_shapes=scratch_shapes,
        compiler_params=pltpu.CompilerParams(vmem_limit_bytes=12 * 2**20),
        cost_estimate=pl.CostEstimate(flops=flops, bytes_accessed=nbytes, transcendentals=0),
    )


def fetched(source, held, sem):
    copy = pltpu.make_async_copy(source, held, sem)
    copy.start()
    copy.wait()
    return held[...]


def scaled(values):
    largest = jnp.maximum(jnp.max(jnp.abs(values), keepdims=True), 1e-30)
    exponent = jnp.floor(jnp.log(largest) * (1 / math.log(2.0))) - TOP
    return values * jnp.exp2(-exponent), exponent


def put_exponent(out, exponent):
    rows = out.shape[1] - EXTRA
    out[:, rows:, :] = jnp.broadcast_to(exponent.reshape(1, 1, 1), (out.shape[0], EXTRA, out.shape[2]))


def split_kernel(proj, out):
    proj, exponent = scaled(proj[...])
    size = out.shape[2]
    for piece in range(out.shape[0]):
        out[piece, :COLS, :] = proj[:, piece * size : (piece + 1) * size]
    put_exponent(out, exponent)


def shrink_kernel(halves, table, lam_space, lam_time, out):
    total = sum(halves[half, :COLS, :] * jnp.exp2(halves[half, COLS : COLS + 1, :]) for half in range(halves.shape[0]))
    diagonal = lax.broadcasted_iota(jnp.int32, (MONTHS, MONTHS), 0) == lax.broadcasted_iota(jnp.int32, (MONTHS, MONTHS), 1)
    time = jnp.sum(jnp.where(diagonal, lam_time[...], 0.0), axis=1, keepdims=True)
    lines = total.shape[1] // lam_space.shape[1]
    space = [lam_space[pl.ds(lax.axis_index(PAIR) * lines + line, 1), :] for line in range(lines)]
    gain = jnp.concatenate([time] * VARS, axis=0) * jnp.concatenate(space, axis=1)
    gain = gain / (gain + 1.0)
    spec = jnp.dot(table[...], total, precision=lax.Precision.HIGHEST, preferred_element_type=jnp.float32)
    back = lax.dot_general(
        spec * gain,
        table[...],
        (((0,), (0,)), ((), ())),
        precision=lax.Precision.HIGHEST,
        preferred_element_type=jnp.float32,
    )
    out[...] = back.astype(jnp.bfloat16)


def smooth_kernel(far, eigvec, coeffs, out, held, sem):
    part, exponent = scaled(jnp.dot(fetched(eigvec, held, sem), coeffs[...], preferred_element_type=jnp.float32))
    size = part.shape[0] // (out.shape[0] * far)
    for block in range(part.shape[0] // size):
        piece = block // (2 * far) * 2 + block % 2
        start = block // 2 % far * size
        out[piece, start : start + size, :] = part[block * size : (block + 1) * size]
    put_exponent(out, exponent)


def gather(block, axes):
    size = lax.axis_size(axes)
    copies = jnp.broadcast_to(block, (size,) + block.shape)
    return lax.all_to_all(copies, axes, 0, 0).reshape((size * block.shape[0],) + block.shape[1:])


def exchange(pieces, axes):
    got = lax.all_to_all(pieces.astype(jnp.float16), axes, 0, 0).astype(jnp.float32)
    rows = got.shape[1] - EXTRA
    return got[:, :rows], got[:, rows : rows + 1]


def shards(observed, prior_mean, missing, eigvec, lam_space, lam_time):
    stations, eigs = eigvec.shape
    pieces = lax.axis_size(PAIR)
    share = eigs // pieces
    flops = 2 * stations * eigs * COLS
    nbytes = 2 * stations * eigs
    filled = jnp.where(missing == 1, prior_mean, observed)
    across, far, near = lax.axis_size("x"), lax.axis_size("za"), lax.axis_size("zc")
    filled = gather(gather(filled, "za"), NEAR).reshape(across, near, far, -1, COLS)
    filled = filled.transpose(0, 2, 1, 3, 4).reshape(stations, COLS)
    proj = lax.dot_general(filled, eigvec, (((0,), (0,)), ((), ())), preferred_element_type=jnp.float32)
    split = kernel_call(
        split_kernel, jax.ShapeDtypeStruct((pieces, COLS + EXTRA, share), jnp.float32), [VMEM], eigs * COLS, 8 * eigs * COLS
    )(proj)
    terms, exponents = exchange(split, PAIR)
    top = exponents.max(0) + math.log2(pieces)
    half = jnp.concatenate([(terms * jnp.exp2(exponents - top)).sum(0), jnp.broadcast_to(top, (EXTRA, share))])
    halves = lax.all_gather(half.astype(jnp.float16), "zh").astype(jnp.float32)
    coeffs = kernel_call(
        shrink_kernel, jax.ShapeDtypeStruct((share, COLS), jnp.bfloat16), [VMEM] * 4, 4 * COLS * COLS * share, COLS * COLS * 8
    )(halves, cosine_blocks(), lam_space.reshape(-1, COLS), lam_time.reshape(1, MONTHS))
    scratch = [pltpu.VMEM(eigvec.shape, eigvec.dtype), pltpu.SemaphoreType.DMA]
    part = kernel_call(
        functools.partial(smooth_kernel, far),
        jax.ShapeDtypeStruct((across * near, stations // (across * near) + EXTRA, COLS), jnp.float32),
        [ANY, VMEM],
        flops,
        nbytes,
        scratch,
    )(eigvec, gather(coeffs, PAIR))
    terms, exponents = exchange(part, NEAR)
    joined = (terms * jnp.exp2(exponents)).sum(0).astype(jnp.bfloat16).reshape(far, -1, COLS)
    return lax.all_to_all(joined, "za", 0, 0).astype(jnp.float32).sum(0)


def solution(mesh):
    fine = Mesh(mesh.devices.reshape(4, 2, 2, 4, 4, 2), ROW + COL)
    rows = P(ROW + COL, None)
    in_specs = (rows, rows, rows, P(ROW, COL), P(COL), P())
    return jax.shard_map(shards, mesh=fine, in_specs=in_specs, out_specs=rows, check_vma=False)
```

```python
import functools
import math

import jax
import jax.numpy as jnp
import numpy as np
from jax import lax
from jax.experimental import pallas as pl
from jax.experimental.pallas import tpu as pltpu
from jax.sharding import Mesh
from jax.sharding import PartitionSpec as P

MONTHS = 32
VARS = 4
COLS = MONTHS * VARS
ROW = ("y", "zh", "core")
COL = ("x", "za", "zc")
NEAR = ("x", "zc")
PAIR = ("y", "core")
EXTRA = 8
TOP = 14
VMEM = pl.BlockSpec(memory_space=pltpu.VMEM)
ANY = pl.BlockSpec(memory_space=pl.ANY)


def cosine_blocks():
    freq = np.arange(MONTHS)[:, None]
    month = np.arange(MONTHS)[None, :]
    table = np.cos(math.pi * (month + 0.5) * freq / MONTHS) * math.sqrt(2.0 / MONTHS)
    table[0] /= math.sqrt(2.0)
    return np.kron(np.eye(VARS), table).astype(np.float32)


def kernel_call(body, out_shape, in_specs, flops, nbytes, scratch_shapes=()):
    return pl.pallas_call(
        body,
        out_shape=out_shape,
        in_specs=in_specs,
        out_specs=VMEM,
        scratch_shapes=scratch_shapes,
        compiler_params=pltpu.CompilerParams(vmem_limit_bytes=12 * 2**20),
        cost_estimate=pl.CostEstimate(flops=flops, bytes_accessed=nbytes, transcendentals=0),
    )


def fetched(source, held, sem):
    copy = pltpu.make_async_copy(source, held, sem)
    copy.start()
    copy.wait()
    return held[...]


def scaled(values):
    largest = jnp.maximum(jnp.max(jnp.abs(values), keepdims=True), 1e-30)
    exponent = jnp.floor(jnp.log(largest) * (1 / math.log(2.0))) - TOP
    return values * jnp.exp2(-exponent), exponent


def put_exponent(out, exponent):
    rows = out.shape[1] - EXTRA
    out[:, rows:, :] = jnp.broadcast_to(exponent.reshape(1, 1, 1), (out.shape[0], EXTRA, out.shape[2]))


def split_kernel(proj, out):
    proj, exponent = scaled(proj[...])
    size = out.shape[2]
    for piece in range(out.shape[0]):
        out[piece, :COLS, :] = proj[:, piece * size : (piece + 1) * size]
    put_exponent(out, exponent)


def shrink_kernel(halves, table, lam_space, lam_time, out):
    total = sum(halves[half, :COLS, :] * jnp.exp2(halves[half, COLS : COLS + 1, :]) for half in range(halves.shape[0]))
    diagonal = lax.broadcasted_iota(jnp.int32, (MONTHS, MONTHS), 0) == lax.broadcasted_iota(jnp.int32, (MONTHS, MONTHS), 1)
    time = jnp.sum(jnp.where(diagonal, lam_time[...], 0.0), axis=1, keepdims=True)
    lines = total.shape[1] // lam_space.shape[1]
    space = [lam_space[pl.ds(lax.axis_index(PAIR) * lines + line, 1), :] for line in range(lines)]
    gain = jnp.concatenate([time] * VARS, axis=0) * jnp.concatenate(space, axis=1)
    gain = gain / (gain + 1.0)
    spec = jnp.dot(table[...], total, precision=lax.Precision.HIGHEST, preferred_element_type=jnp.float32)
    back = lax.dot_general(
        spec * gain,
        table[...],
        (((0,), (0,)), ((), ())),
        precision=lax.Precision.HIGHEST,
        preferred_element_type=jnp.float32,
    )
    out[...] = back.astype(jnp.bfloat16)


def smooth_kernel(far, eigvec, coeffs, out, held, sem):
    part, exponent = scaled(jnp.dot(fetched(eigvec, held, sem), coeffs[...], preferred_element_type=jnp.float32))
    size = part.shape[0] // (out.shape[0] * far)
    for block in range(part.shape[0] // size):
        piece = block // (2 * far) * 2 + block % 2
        start = block // 2 % far * size
        out[piece, start : start + size, :] = part[block * size : (block + 1) * size]
    put_exponent(out, exponent)


def gather(block, axes):
    size = lax.axis_size(axes)
    copies = jnp.broadcast_to(block, (size,) + block.shape)
    return lax.all_to_all(copies, axes, 0, 0).reshape((size * block.shape[0],) + block.shape[1:])


def exchange(pieces, axes):
    got = lax.all_to_all(pieces.astype(jnp.float16), axes, 0, 0).astype(jnp.float32)
    rows = got.shape[1] - EXTRA
    return got[:, :rows], got[:, rows : rows + 1]


def scaled_sum(terms, exponents):
    top = exponents.max(0) + math.log2(terms.shape[0])
    return (terms * jnp.exp2(exponents - top)).sum(0), top


def shards(observed, prior_mean, missing, eigvec, lam_space, lam_time):
    stations, eigs = eigvec.shape
    pieces = lax.axis_size(PAIR)
    share = eigs // pieces
    flops = 2 * stations * eigs * COLS
    nbytes = 2 * stations * eigs
    filled = jnp.where(missing == 1, prior_mean, observed)
    across, far, near = lax.axis_size("x"), lax.axis_size("za"), lax.axis_size("zc")
    filled = gather(gather(filled, "za"), NEAR).reshape(across, near, far, -1, COLS)
    filled = filled.transpose(0, 2, 1, 3, 4).reshape(stations, COLS)
    proj = lax.dot_general(filled, eigvec, (((0,), (0,)), ((), ())), preferred_element_type=jnp.float32)
    split = kernel_call(
        split_kernel, jax.ShapeDtypeStruct((pieces, COLS + EXTRA, share), jnp.float32), [VMEM], eigs * COLS, 8 * eigs * COLS
    )(proj)
    half, top = scaled_sum(*exchange(split, PAIR))
    half = jnp.concatenate([half, jnp.broadcast_to(top, (EXTRA, share))])
    halves = lax.all_gather(half.astype(jnp.float16), "zh").astype(jnp.float32)
    coeffs = kernel_call(
        shrink_kernel, jax.ShapeDtypeStruct((share, COLS), jnp.bfloat16), [VMEM] * 4, 4 * COLS * COLS * share, COLS * COLS * 8
    )(halves, cosine_blocks(), lam_space.reshape(-1, COLS), lam_time.reshape(1, MONTHS))
    scratch = [pltpu.VMEM(eigvec.shape, eigvec.dtype), pltpu.SemaphoreType.DMA]
    part = kernel_call(
        functools.partial(smooth_kernel, far),
        jax.ShapeDtypeStruct((across * near, stations // (across * near) + EXTRA, COLS), jnp.float32),
        [ANY, VMEM],
        flops,
        nbytes,
        scratch,
    )(eigvec, gather(coeffs, PAIR))
    joined, top = scaled_sum(*exchange(part, NEAR))
    joined = joined.reshape(far, -1, COLS)
    terms, exponents = exchange(jnp.concatenate([joined, jnp.broadcast_to(top, (far, EXTRA, COLS))], axis=1), "za")
    return (terms * jnp.exp2(exponents)).sum(0)


def solution(mesh):
    fine = Mesh(mesh.devices.reshape(4, 2, 2, 4, 4, 2), ROW + COL)
    rows = P(ROW + COL, None)
    in_specs = (rows, rows, rows, P(ROW, COL), P(COL), P())
    return jax.shard_map(shards, mesh=fine, in_specs=in_specs, out_specs=rows, check_vma=False)
```

```python
import functools
import math

import jax
import jax.numpy as jnp
import numpy as np
from jax import lax
from jax.experimental import pallas as pl
from jax.experimental.pallas import tpu as pltpu
from jax.sharding import Mesh
from jax.sharding import PartitionSpec as P

MONTHS = 32
VARS = 4
COLS = MONTHS * VARS
ROW = ("y", "zh", "core")
COL = ("x", "za", "zc")
NEAR = ("x", "zc")
PAIR = ("y", "core")
EXTRA = 8
TOP = 14
VMEM = pl.BlockSpec(memory_space=pltpu.VMEM)
ANY = pl.BlockSpec(memory_space=pl.ANY)


def cosine_blocks():
    freq = np.arange(MONTHS)[:, None]
    month = np.arange(MONTHS)[None, :]
    table = np.cos(math.pi * (month + 0.5) * freq / MONTHS) * math.sqrt(2.0 / MONTHS)
    table[0] /= math.sqrt(2.0)
    return np.kron(np.eye(VARS), table).astype(np.float32)


def kernel_call(body, out_shape, in_specs, flops, nbytes, scratch_shapes=()):
    return pl.pallas_call(
        body,
        out_shape=out_shape,
        in_specs=in_specs,
        out_specs=VMEM,
        scratch_shapes=scratch_shapes,
        compiler_params=pltpu.CompilerParams(vmem_limit_bytes=12 * 2**20),
        cost_estimate=pl.CostEstimate(flops=flops, bytes_accessed=nbytes, transcendentals=0),
    )


def fetched(source, held, sem):
    copy = pltpu.make_async_copy(source, held, sem)
    copy.start()
    copy.wait()
    return held[...]


def exponent_of(values):
    largest = jnp.maximum(jnp.max(jnp.abs(values), keepdims=True), 1e-30)
    return jnp.floor(jnp.log(largest) * (1 / math.log(2.0))) - TOP


def put_exponent(out, exponent):
    rows = out.shape[1] - EXTRA
    out[:, rows:, :] = jnp.broadcast_to(exponent.reshape(1, 1, 1), (out.shape[0], EXTRA, out.shape[2]))


def split_kernel(proj, out):
    size = out.shape[2]
    for piece in range(out.shape[0]):
        out[piece, :COLS, :] = proj[:, piece * size : (piece + 1) * size]
    put_exponent(out, exponent_of(proj[...]))


def shrink_kernel(halves, table, lam_space, lam_time, out):
    total = sum(halves[half, :COLS, :] * jnp.exp2(halves[half, COLS : COLS + 1, :]) for half in range(halves.shape[0]))
    diagonal = lax.broadcasted_iota(jnp.int32, (MONTHS, MONTHS), 0) == lax.broadcasted_iota(jnp.int32, (MONTHS, MONTHS), 1)
    time = jnp.sum(jnp.where(diagonal, lam_time[...], 0.0), axis=1, keepdims=True)
    lines = total.shape[1] // lam_space.shape[1]
    space = [lam_space[pl.ds(lax.axis_index(PAIR) * lines + line, 1), :] for line in range(lines)]
    gain = jnp.concatenate([time] * VARS, axis=0) * jnp.concatenate(space, axis=1)
    gain = gain / (gain + 1.0)
    spec = jnp.dot(table[...], total, precision=lax.Precision.HIGHEST, preferred_element_type=jnp.float32)
    back = lax.dot_general(
        spec * gain,
        table[...],
        (((0,), (0,)), ((), ())),
        precision=lax.Precision.HIGHEST,
        preferred_element_type=jnp.float32,
    )
    out[...] = back.astype(jnp.bfloat16)


def smooth_kernel(far, eigvec, coeffs, out, held, sem):
    part = jnp.dot(fetched(eigvec, held, sem), coeffs[...], preferred_element_type=jnp.float32)
    size = part.shape[0] // (out.shape[0] * far)
    for block in range(part.shape[0] // size):
        piece = block // (2 * far) * 2 + block % 2
        start = block // 2 % far * size
        out[piece, start : start + size, :] = part[block * size : (block + 1) * size]
    put_exponent(out, exponent_of(part))


def gather(block, axes):
    size = lax.axis_size(axes)
    copies = jnp.broadcast_to(block, (size,) + block.shape)
    return lax.all_to_all(copies, axes, 0, 0).reshape((size * block.shape[0],) + block.shape[1:])


def exchange(pieces, axes):
    got = lax.all_to_all(pieces.astype(jnp.float16), axes, 0, 0).astype(jnp.float32)
    rows = got.shape[1] - EXTRA
    return got[:, :rows], got[:, rows : rows + 1]


def scaled(pieces):
    rows = pieces.shape[1] - EXTRA
    row = lax.broadcasted_iota(jnp.int32, pieces.shape, 1)
    return jnp.where(row < rows, pieces * jnp.exp2(-pieces[:, rows : rows + 1]), pieces)


def scaled_sum(terms, exponents):
    top = exponents.max(0) + math.log2(terms.shape[0])
    return (terms * jnp.exp2(exponents - top)).sum(0), top


def shards(observed, prior_mean, missing, eigvec, lam_space, lam_time):
    stations, eigs = eigvec.shape
    pieces = lax.axis_size(PAIR)
    share = eigs // pieces
    flops = 2 * stations * eigs * COLS
    nbytes = 2 * stations * eigs
    filled = jnp.where(missing == 1, prior_mean, observed)
    across, far, near = lax.axis_size("x"), lax.axis_size("za"), lax.axis_size("zc")
    filled = gather(gather(filled, "za"), NEAR).reshape(across, near, far, -1, COLS)
    filled = filled.transpose(0, 2, 1, 3, 4).reshape(stations, COLS)
    proj = lax.dot_general(filled, eigvec, (((0,), (0,)), ((), ())), preferred_element_type=jnp.float32)
    split = kernel_call(
        split_kernel, jax.ShapeDtypeStruct((pieces, COLS + EXTRA, share), jnp.float32), [VMEM], eigs * COLS, 8 * eigs * COLS
    )(proj)
    half, top = scaled_sum(*exchange(scaled(split), PAIR))
    half = jnp.concatenate([half, jnp.broadcast_to(top, (EXTRA, share))])
    halves = lax.all_gather(half.astype(jnp.float16), "zh").astype(jnp.float32)
    coeffs = kernel_call(
        shrink_kernel, jax.ShapeDtypeStruct((share, COLS), jnp.bfloat16), [VMEM] * 4, 4 * COLS * COLS * share, COLS * COLS * 8
    )(halves, cosine_blocks(), lam_space.reshape(-1, COLS), lam_time.reshape(1, MONTHS))
    scratch = [pltpu.VMEM(eigvec.shape, eigvec.dtype), pltpu.SemaphoreType.DMA]
    part = kernel_call(
        functools.partial(smooth_kernel, far),
        jax.ShapeDtypeStruct((across * near, stations // (across * near) + EXTRA, COLS), jnp.float32),
        [ANY, VMEM],
        flops,
        nbytes,
        scratch,
    )(eigvec, gather(coeffs, PAIR))
    joined, top = scaled_sum(*exchange(scaled(part), NEAR))
    joined = joined.reshape(far, -1, COLS)
    terms, exponents = exchange(jnp.concatenate([joined, jnp.broadcast_to(top, (far, EXTRA, COLS))], axis=1), "za")
    return (terms * jnp.exp2(exponents)).sum(0)


def solution(mesh):
    fine = Mesh(mesh.devices.reshape(4, 2, 2, 4, 4, 2), ROW + COL)
    rows = P(ROW + COL, None)
    in_specs = (rows, rows, rows, P(ROW, COL), P(COL), P())
    return jax.shard_map(shards, mesh=fine, in_specs=in_specs, out_specs=rows, check_vma=False)
```

```python
import functools
import math

import jax
import jax.numpy as jnp
import numpy as np
from jax import lax
from jax.experimental import pallas as pl
from jax.experimental.pallas import tpu as pltpu
from jax.sharding import Mesh
from jax.sharding import PartitionSpec as P

MONTHS = 32
VARS = 4
COLS = MONTHS * VARS
ROW = ("y", "zh", "core")
COL = ("x", "za", "zc")
NEAR = ("x", "zc")
PAIR = ("y", "core")
EXTRA = 8
TOP = 14
VMEM = pl.BlockSpec(memory_space=pltpu.VMEM)
ANY = pl.BlockSpec(memory_space=pl.ANY)


def cosine_blocks():
    freq = np.arange(MONTHS)[:, None]
    month = np.arange(MONTHS)[None, :]
    table = np.cos(math.pi * (month + 0.5) * freq / MONTHS) * math.sqrt(2.0 / MONTHS)
    table[0] /= math.sqrt(2.0)
    return np.kron(np.eye(VARS), table).astype(np.float32)


def kernel_call(body, out_shape, in_specs, flops, nbytes, scratch_shapes=()):
    return pl.pallas_call(
        body,
        out_shape=out_shape,
        in_specs=in_specs,
        out_specs=VMEM,
        scratch_shapes=scratch_shapes,
        compiler_params=pltpu.CompilerParams(vmem_limit_bytes=8 * 2**20),
        cost_estimate=pl.CostEstimate(flops=flops, bytes_accessed=nbytes, transcendentals=0),
    )


def fetched(source, held, sem):
    copy = pltpu.make_async_copy(source, held, sem)
    copy.start()
    copy.wait()
    return held[...]


def scaled(values):
    largest = jnp.maximum(jnp.max(jnp.abs(values), keepdims=True), 1e-30)
    exponent = jnp.floor(jnp.log(largest) * (1 / math.log(2.0))) - TOP
    return values * jnp.exp2(-exponent), exponent


def put_exponent(out, exponent):
    rows = out.shape[1] - EXTRA
    out[:, rows:, :] = jnp.broadcast_to(exponent.reshape(1, 1, 1), (out.shape[0], EXTRA, out.shape[2]))


def split_kernel(proj, out):
    proj, exponent = scaled(proj[...])
    size = out.shape[2]
    for piece in range(out.shape[0]):
        out[piece, :COLS, :] = proj[:, piece * size : (piece + 1) * size]
    put_exponent(out, exponent)


def shrink_kernel(halves, table, lam_space, lam_time, out):
    total = sum(halves[half, :COLS, :] * jnp.exp2(halves[half, COLS : COLS + 1, :]) for half in range(halves.shape[0]))
    diagonal = lax.broadcasted_iota(jnp.int32, (MONTHS, MONTHS), 0) == lax.broadcasted_iota(jnp.int32, (MONTHS, MONTHS), 1)
    time = jnp.sum(jnp.where(diagonal, lam_time[...], 0.0), axis=1, keepdims=True)
    lines = total.shape[1] // lam_space.shape[1]
    space = [lam_space[pl.ds(lax.axis_index(PAIR) * lines + line, 1), :] for line in range(lines)]
    gain = jnp.concatenate([time] * VARS, axis=0) * jnp.concatenate(space, axis=1)
    gain = gain / (gain + 1.0)
    spec = jnp.dot(table[...], total, precision=lax.Precision.HIGHEST, preferred_element_type=jnp.float32)
    back = lax.dot_general(
        spec * gain,
        table[...],
        (((0,), (0,)), ((), ())),
        precision=lax.Precision.HIGHEST,
        preferred_element_type=jnp.float32,
    )
    out[...] = back.astype(jnp.bfloat16)


def smooth_kernel(far, eigvec, coeffs, out, held, sem):
    part, exponent = scaled(jnp.dot(fetched(eigvec, held, sem), coeffs[...], preferred_element_type=jnp.float32))
    size = part.shape[0] // (out.shape[0] * far)
    for block in range(part.shape[0] // size):
        piece = block // (2 * far) * 2 + block % 2
        start = block // 2 % far * size
        out[piece, start : start + size, :] = part[block * size : (block + 1) * size]
    put_exponent(out, exponent)


def gather(block, axes):
    size = lax.axis_size(axes)
    copies = jnp.broadcast_to(block, (size,) + block.shape)
    return lax.all_to_all(copies, axes, 0, 0).reshape((size * block.shape[0],) + block.shape[1:])


def exchange(pieces, axes):
    got = lax.all_to_all(pieces.astype(jnp.float16), axes, 0, 0).astype(jnp.float32)
    rows = got.shape[1] - EXTRA
    return got[:, :rows], got[:, rows : rows + 1]


def scaled_sum(terms, exponents):
    top = exponents.max(0) + math.log2(terms.shape[0])
    return (terms * jnp.exp2(exponents - top)).sum(0), top


def shards(observed, prior_mean, missing, eigvec, lam_space, lam_time):
    stations, eigs = eigvec.shape
    pieces = lax.axis_size(PAIR)
    share = eigs // pieces
    flops = 2 * stations * eigs * COLS
    nbytes = 2 * stations * eigs
    filled = jnp.where(missing == 1, prior_mean, observed)
    across, far, near = lax.axis_size("x"), lax.axis_size("za"), lax.axis_size("zc")
    filled = gather(gather(filled, "za"), NEAR).reshape(across, near, far, -1, COLS)
    filled = filled.transpose(0, 2, 1, 3, 4).reshape(stations, COLS)
    proj = lax.dot_general(filled, eigvec, (((0,), (0,)), ((), ())), preferred_element_type=jnp.float32)
    split = kernel_call(
        split_kernel, jax.ShapeDtypeStruct((pieces, COLS + EXTRA, share), jnp.float32), [VMEM], eigs * COLS, 8 * eigs * COLS
    )(proj)
    half, top = scaled_sum(*exchange(split, PAIR))
    half = jnp.concatenate([half, jnp.broadcast_to(top, (EXTRA, share))])
    halves = lax.all_gather(half.astype(jnp.float16), "zh").astype(jnp.float32)
    coeffs = kernel_call(
        shrink_kernel, jax.ShapeDtypeStruct((share, COLS), jnp.bfloat16), [VMEM] * 4, 4 * COLS * COLS * share, COLS * COLS * 8
    )(halves, cosine_blocks(), lam_space.reshape(-1, COLS), lam_time.reshape(1, MONTHS))
    scratch = [pltpu.VMEM(eigvec.shape, eigvec.dtype), pltpu.SemaphoreType.DMA]
    part = kernel_call(
        functools.partial(smooth_kernel, far),
        jax.ShapeDtypeStruct((across * near, stations // (across * near) + EXTRA, COLS), jnp.float32),
        [ANY, VMEM],
        flops,
        nbytes,
        scratch,
    )(eigvec, gather(coeffs, PAIR))
    joined, top = scaled_sum(*exchange(part, NEAR))
    joined = joined.reshape(far, -1, COLS)
    terms, exponents = exchange(jnp.concatenate([joined, jnp.broadcast_to(top, (far, EXTRA, COLS))], axis=1), "za")
    return (terms * jnp.exp2(exponents)).sum(0)


def solution(mesh):
    fine = Mesh(mesh.devices.reshape(4, 2, 2, 4, 4, 2), ROW + COL)
    rows = P(ROW + COL, None)
    in_specs = (rows, rows, rows, P(ROW, COL), P(COL), P())
    return jax.shard_map(shards, mesh=fine, in_specs=in_specs, out_specs=rows, check_vma=False)
```
